32 devices in a mesh: ctx: 4 (over y, x), ep: 8 (over z, core).
Axes of the slice: x: 2, y: 2, z: 4, core: 2. Of those that a mesh axis runs over, the one named last changes fastest.
Arguments:
- latent_cache: bfloat16 [2048, 576], P(('ctx', 'ep'))
- prefill_query: bfloat16 [256, 32, 576], P('ctx', 'ep')
- prompt_lengths: int32 [2], replicated, may hold values from 1 to 1536, 2048 in all
- group_of: int32 [4], replicated, may hold values from 0 to 1, as said below
- decode_latent: bfloat16 [4, 2, 64, 576], P('ctx')
- decode_query: bfloat16 [4, 2, 64, 32, 576], P('ctx', None, None, 'ep')
Outputs:
- prefill_out: bfloat16 [256, 32, 512], P('ctx', 'ep')
- decode_out: bfloat16 [4, 2, 64, 32, 512], P('ctx', None, None, 'ep')
The draws below stay inside these ranges and needn't reach their ends.
Inputs may be any that keep to these rules, and one draw needn't show every extreme that they name: `prompt_lengths`: the 2 prompt lengths add up to 2048, and the longest is at most 1536. `group_of`: every prompt is decoded by exactly 2 groups.
All inputs are finite; a program needn't handle non-finite values.
Results may differ from the reference program's by a relative error of at most 0.004.
Values may be sent and summed in bfloat16 or wider, within the bound.
A program may use at most 128 MiB of HBM per device.

```python
import math
import jax
import jax.numpy as jnp
import numpy as np
from jax import lax

LAT = 512
CW = 576
HEADS = 32
REQS = 2
CTX = 2048
QROWS = 256
SPAN = 128
GROUPS = 4
CAP = 1536
STEPS = 2
DEC_ROWS = 64


def cache_values(key):
    return jax.random.normal(jax.random.fold_in(key, 200), (CTX, CW), jnp.float32)


def decode_values(key):
    return jax.random.normal(jax.random.fold_in(key, 100), (GROUPS, STEPS, DEC_ROWS, CW), jnp.float32)


def draw_latent_cache(key, part):
    values = cache_values(key)
    return values.astype(jnp.bfloat16)


def draw_group_of(key, part):
    key = jax.random.fold_in(key, 7)
    order = jax.random.permutation(key, GROUPS)
    return (order % REQS).astype(jnp.int32)


def draw_prefill_query(key, part):
    key = jax.random.fold_in(key, 2)
    query = 0.6 * jax.random.normal(key, (QROWS, HEADS, CW), jnp.float32)
    return query.astype(jnp.bfloat16)


def draw_decode_latent(key, part):
    values = decode_values(key)
    return values.astype(jnp.bfloat16)


def draw_decode_query(key, part):
    key = jax.random.fold_in(key, 4)
    query = 0.6 * jax.random.normal(key, (GROUPS, STEPS, DEC_ROWS, HEADS, CW), jnp.float32)
    return query.astype(jnp.bfloat16)


def split_up(number_of, total, reach, slope):
    loads = [(1 << 20) // math.isqrt(standing ** slope) + 1 for standing in range(2, number_of + 1)]
    spare, counts = total - reach - (number_of - 1), [1] * (number_of - 1)
    while spare > 0:
        free = [i for i in range(number_of - 1) if counts[i] < reach]
        whole, budget = sum([loads[i] for i in free]), spare
        for i in free:
            more = min(reach - counts[i], max(1, budget * loads[i] // whole), spare)
            counts[i] = counts[i] + more
            spare = spare - more
    return np.array([reach] + counts)


def ragged_sizes(own_key, amount, total, reach, slope):
    if amount == 2:
        one = jax.random.randint(own_key, (), max(1, total - reach), min(reach, total - 1) + 1)
        return jnp.stack([one, total - one])
    sizes = jnp.asarray(split_up(amount, total, reach, slope), jnp.int32)
    pairs = (amount - 1) // 2
    donor, taker = sizes[1:1 + 2 * pairs:2], sizes[2:2 + 2 * pairs:2]
    margin = jnp.minimum(donor - 1, reach - taker)
    passed = jax.random.randint(jax.random.fold_in(own_key, 1), (pairs,), 0, 1 << 20) % (margin + 1)
    sizes = sizes.at[1:1 + 2 * pairs:2].set(donor - passed).at[2:2 + 2 * pairs:2].set(taker + passed)
    return sizes[jax.random.permutation(jax.random.fold_in(own_key, 2), amount)]


def setup_inputs(seed: int = 0) -> dict:
    splits = jax.random.split(jax.random.key(seed), 7)
    return {
        "latent_cache": draw_latent_cache(jax.random.fold_in(splits[6], 71), 0),
        "prefill_query": draw_prefill_query(jax.random.fold_in(splits[6], 71), 0),
        "prompt_lengths": ragged_sizes(splits[2], REQS, CTX, CAP, 2).astype(jnp.int32),
        "group_of": draw_group_of(jax.random.fold_in(splits[6], 71), 0),
        "decode_latent": draw_decode_latent(jax.random.fold_in(splits[6], 71), 0),
        "decode_query": draw_decode_query(jax.random.fold_in(splits[6], 71), 0),
    }


SCALE = 192 ** -0.5
FLOOR = -1.0e30


def decode_group(prefix, live, new_rows, queries):
    results = []
    for step in range(STEPS):
        query = queries[step]
        count = query.shape[0]
        heads = query.shape[1]
        flat = query.reshape(count * heads, CW)
        prefix_scores = jnp.dot(flat, prefix.T, preferred_element_type=jnp.float32) * SCALE
        prefix_scores = jnp.where(live[None, :], prefix_scores, FLOOR).reshape(count, heads, CAP)
        own = new_rows[: step + 1]
        own_scores = jnp.einsum("rhc,src->rhs", query.astype(jnp.float32), own.astype(jnp.float32)) * SCALE
        top = jnp.maximum(jnp.max(prefix_scores, axis=2), jnp.max(own_scores, axis=2))
        prefix_weights = jnp.where(live[None, None, :], jnp.exp(prefix_scores - top[:, :, None]), 0.0)
        own_weights = jnp.exp(own_scores - top[:, :, None])
        total = jnp.sum(prefix_weights, axis=2) + jnp.sum(own_weights, axis=2)
        mixed = jnp.dot(prefix_weights.astype(jnp.bfloat16).reshape(count * heads, CAP), prefix[:, :LAT], preferred_element_type=jnp.float32).reshape(count, heads, LAT)
        rounded_own = lax.optimization_barrier(own_weights.astype(jnp.bfloat16))
        mixed = mixed + jnp.einsum("rhs,src->rhc", rounded_own.astype(jnp.float32), own[:, :, :LAT].astype(jnp.float32))
        results.append((mixed / total[:, :, None]).astype(jnp.bfloat16))
    return jnp.stack(results)


def reference(latent_cache, prefill_query, prompt_lengths, group_of, decode_latent, decode_query):
    ends = jnp.cumsum(prompt_lengths).astype(jnp.int32)
    starts = (ends - prompt_lengths).astype(jnp.int32)
    positions = jnp.arange(CTX, dtype=jnp.int32)
    segment = jnp.sum((positions[:, None] >= ends[None, :]).astype(jnp.int32), axis=1)
    query_ids = jnp.arange(QROWS, dtype=jnp.int32)
    query_req = (query_ids // SPAN).astype(jnp.int32)
    request_ids = jnp.arange(REQS, dtype=jnp.int32)
    query_end = jnp.sum(jnp.where(query_req[:, None] == request_ids[None, :], ends[None, :], 0), axis=1).astype(jnp.int32)
    query_pos = (query_end - SPAN + query_ids % SPAN).astype(jnp.int32)
    allowed = (query_req[:, None] == segment[None, :]) & (positions[None, :] <= query_pos[:, None])
    values = latent_cache[:, :LAT]

    def one_head(query):
        scores = jnp.dot(query, latent_cache.T, preferred_element_type=jnp.float32) * SCALE
        scores = jnp.where(allowed, scores, FLOOR)
        top = jnp.max(scores, axis=1, keepdims=True)
        weights = jnp.where(allowed, jnp.exp(scores - top), 0.0)
        total = jnp.sum(weights, axis=1, keepdims=True)
        mixed = jnp.dot(weights.astype(jnp.bfloat16), values, preferred_element_type=jnp.float32)
        return (mixed / total).astype(jnp.bfloat16)

    prefill_out = jnp.swapaxes(lax.map(one_head, jnp.swapaxes(prefill_query, 0, 1)), 0, 1)

    owner = group_of[:, None] == request_ids[None, :]
    group_start = jnp.sum(jnp.where(owner, starts[None, :], 0), axis=1).astype(jnp.int32)
    group_length = jnp.sum(jnp.where(owner, prompt_lengths[None, :], 0), axis=1).astype(jnp.int32)
    padded = jnp.concatenate([latent_cache, jnp.zeros((CAP, CW), jnp.bfloat16)], axis=0)

    def one_group(items):
        start, length, new_rows, queries = items
        prefix = lax.dynamic_slice_in_dim(padded, start.astype(jnp.int32), CAP, 0)
        live = jnp.arange(CAP, dtype=jnp.int32) < length
        return decode_group(prefix, live, new_rows, queries)

    decode_out = lax.map(one_group, (group_start, group_length, decode_latent, decode_query))
    return (prefill_out, decode_out)
```

```python
import functools
import math

import jax
import jax.numpy as jnp
from jax import lax
from jax.experimental import pallas as pl
from jax.experimental.pallas import tpu as pltpu
from jax.sharding import PartitionSpec as P

LAT = 512
SCALE = 192 ** (-0.5)
RATE = SCALE * math.log2(math.e)
FLOOR = -1e30
MESH = pl.DeviceIdType.MESH


def kernel(
    sizes,
    lengths_ref,
    group_ref,
    latent_ref,
    pq_ref,
    dq_ref,
    own_ref,
    pout_ref,
    dout_ref,
    cache,
    queries,
    acc,
    local_sem,
    send_sem,
    recv_sem,
):
    ctx_count, ep_count, heads, steps = sizes
    zs = ep_count // 2
    n2 = 2 if ctx_count % 2 == 0 else 1
    n1 = ctx_count // n2
    rows = latent_ref.shape[0]
    p_rows, d_rows = pq_ref.shape[0], dq_ref.shape[0]
    ctx = lax.axis_index("ctx")
    ep = lax.axis_index("ep")
    core = lax.rem(ep, 2)
    z = ep // 2
    i1, i2 = ctx // n2, lax.rem(ctx, n2)
    turn = core if n1 == n2 else 0
    na, nb = n2, n1
    fine = zs <= 4

    def column(a, b):
        o1 = b + turn * (a - b)
        o2 = a + turn * (b - a)
        return lax.rem(i1 + o1, n1) * n2 + lax.rem(i2 + o2, n2)

    def plane(dz):
        return lax.rem(z + dz, zs)

    sibling = (ctx, ep + 1 - 2 * core)
    z_peers = [(ctx, plane(dz) * 2 + core) for dz in range(1, zs)]
    a_peers = [(column(a, 0), ep) for a in range(1, na)]
    b_peers = [(column(0, b), ep) for b in range(1, nb)]

    barrier = pltpu.get_barrier_semaphore()
    partners = [sibling] + z_peers + a_peers + b_peers
    for peer in partners:
        pl.semaphore_signal(barrier, inc=1, device_id=peer, device_id_type=MESH)

    own_copy = pltpu.make_async_copy(latent_ref, cache.at[ctx, core, z], local_sem.at[0])
    own_copy.start()
    p_copy = pltpu.make_async_copy(pq_ref, queries.at[pl.ds(0, p_rows)], local_sem.at[1])
    p_copy.start()
    d_copy = pltpu.make_async_copy(dq_ref, queries.at[pl.ds(p_rows, d_rows)], local_sem.at[2])
    d_copy.start()
    pl.semaphore_wait(barrier, len(partners))

    sent = []

    def send(source, target, recv, peer):
        copy = pltpu.make_async_remote_copy(
            src_ref=source,
            dst_ref=target,
            send_sem=send_sem.at[len(sent)],
            recv_sem=recv,
            device_id=peer,
            device_id_type=MESH,
        )
        copy.start()
        sent.append(copy)

    def landed(target, recv):
        pltpu.make_async_remote_copy(
            src_ref=target,
            dst_ref=target,
            send_sem=send_sem.at[0],
            recv_sem=recv,
            device_id=sibling,
            device_id_type=MESH,
        ).wait_recv()

    def place(col, side, dz):
        if dz is None:
            return cache.at[col, side], recv_sem.at[col, side, 0]
        return cache.at[col, side, plane(dz)], recv_sem.at[col, side, plane(dz)]

    parts = list(range(zs)) if fine else [None]

    slot, recv = place(ctx, core, 0)
    for peer in z_peers:
        send(latent_ref, slot, recv, peer)

    def forward(source, col, dz, peers):
        target, recv = place(col, core, dz)
        for peer in peers:
            send(target if source is None else source, target, recv, peer)

    def own_column():
        if fine:
            forward(latent_ref, ctx, 0, b_peers + a_peers + [sibling])
            yield
            for dz in range(1, zs):
                landed(*place(ctx, core, dz))
                forward(None, ctx, dz, b_peers + a_peers + [sibling])
        else:
            yield
            for dz in range(1, zs):
                landed(*place(ctx, core, dz))
            forward(None, ctx, None, b_peers + a_peers + [sibling])

    def pass_on(col, peers):
        for dz in parts:
            landed(*place(col, core, dz))
            forward(None, col, dz, peers)

    def await_sibling(col):
        for dz in parts:
            landed(*place(col, 1 - core, dz))

    first = own_column()
    next(first)

    request_count = lengths_ref.shape[0]
    q_count = p_rows // heads
    span = q_count * ctx_count // request_count
    chosen = group_ref[ctx]
    row = lax.broadcasted_iota(jnp.int32, (p_rows, 1), 0)
    query_id = ctx * q_count + row // heads
    low = jnp.zeros((p_rows, 1), jnp.int32)
    high = jnp.zeros((p_rows, 1), jnp.int32)
    d_low = jnp.int32(0)
    d_high = jnp.int32(0)
    end = jnp.int32(0)
    for r in range(request_count):
        start = end
        end = start + lengths_ref[r]
        mine = (query_id >= r * span) & (query_id < (r + 1) * span)
        low = jnp.where(mine, start, low)
        high = jnp.where(mine, end - span + (query_id - r * span), high)
        d_low = jnp.where(chosen == r, start, d_low)
        d_high = jnp.where(chosen == r, end, d_high)

    block = p_rows
    blocks = (p_rows + d_rows) // block
    tops = [None] * blocks
    totals = [None] * blocks

    def lanes(x):
        out = x[:, :128]
        for i in range(1, x.shape[1] // 128):
            out = out + x[:, i * 128 : (i + 1) * 128]
        return out

    def attend(i, keys, allowed):
        span_i = pl.ds(i * block, block)
        scores = lax.dot_general(
            queries[span_i, :], keys, (((1,), (1,)), ((), ())), preferred_element_type=jnp.float32
        )
        scores = jnp.where(allowed, scores, FLOOR)
        top = jnp.max(scores, axis=1, keepdims=True)
        if tops[i] is not None:
            top = jnp.maximum(top, tops[i])
        weights = jnp.exp2((scores - top) * RATE)
        mixed = jnp.dot(
            weights.astype(jnp.bfloat16), keys[:, :LAT], preferred_element_type=jnp.float32
        )
        total = lanes(weights)
        if tops[i] is None:
            acc[span_i, :] = mixed
        else:
            keep = jnp.exp2((tops[i] - top) * RATE)
            acc[span_i, :] = acc[span_i, :] * keep + mixed
            total = total + totals[i] * keep
        tops[i], totals[i] = top, total

    def compute(col, side):
        keys = cache[col, side].reshape(zs * rows, cache.shape[-1])
        lane = lax.broadcasted_iota(jnp.int32, (1, zs * rows), 1)
        pos = col * (rows * ep_count) + (lane // rows * 2 + side) * rows + lane % rows
        attend(0, keys, (pos >= low) & (pos <= high))
        live = (pos >= d_low) & (pos < d_high)
        for i in range(1, blocks):
            attend(i, keys, live)

    p_copy.wait()
    d_copy.wait()
    count = own_ref.shape[0] // steps
    lane = lax.broadcasted_iota(jnp.int32, (1, own_ref.shape[0]), 1)
    for i in range(1, blocks):
        at = lax.broadcasted_iota(jnp.int32, (block, 1), 0) + (i - 1) * block
        token = at // heads
        same = (lane % count == token % count) & (lane // count <= token // count)
        attend(i, own_ref[...], same)

    own_copy.wait()
    for _ in first:
        pass
    compute(ctx, core)
    for a in range(1, na):
        pass_on(column(a, 0), b_peers + [sibling])
    await_sibling(ctx)
    compute(ctx, 1 - core)
    for a in range(1, na):
        compute(column(a, 0), core)
    if n1 == n2:
        theirs = [(b, a) for b in range(nb) for a in range(na) if (a, b) != (0, 0)]
        theirs = [(a, b) for b in range(nb) for a in range(na) if (a, b) != (0, 0)]
        theirs = [(b, a) for (a, b) in theirs]
    else:
        theirs = [(a, b) for b in range(nb) for a in range(na) if (a, b) != (0, 0)]
    mine = [(a, b) for b in range(1, nb) for a in range(na)]
    ahead = len(theirs) - len(mine)
    for a, b in theirs[:ahead]:
        await_sibling(column(a, b))
        compute(column(a, b), 1 - core)
    for (a, b), (c, d) in zip(mine, theirs[ahead:]):
        pass_on(column(a, b), [sibling])
        compute(column(a, b), core)
        await_sibling(column(c, d))
        compute(column(c, d), 1 - core)

    for i in range(blocks):
        total = jnp.sum(totals[i], axis=1, keepdims=True)
        out = (acc[pl.ds(i * block, block), :] / total).astype(jnp.bfloat16)
        if i == 0:
            pout_ref[...] = out
        else:
            dout_ref[pl.ds((i - 1) * block, block), :] = out
    for copy in sent:
        copy.wait_send()


def body(ctx_count, ep_count, latent, prefill_query, lengths, group_of, own, decode_query):
    rows, width = latent.shape
    q_count, heads, _ = prefill_query.shape
    _, steps, count, _, _ = decode_query.shape
    p_rows, d_rows = q_count * heads, steps * count * heads
    zs = ep_count // 2
    n2 = 2 if ctx_count % 2 == 0 else 1
    n1 = ctx_count // n2
    unit = zs if zs <= 4 else 1
    copies = (zs - 1) + unit * ((n2 - 1) + n2 * (n1 - 1) + ctx_count)
    smem = pl.BlockSpec(memory_space=pltpu.SMEM)
    anywhere = pl.BlockSpec(memory_space=pl.ANY)
    vmem = pl.BlockSpec(memory_space=pltpu.VMEM)
    pairs = (p_rows + d_rows) * (rows * ep_count * ctx_count + steps * count)
    prefill, decode = pl.pallas_call(
        functools.partial(kernel, (ctx_count, ep_count, heads, steps)),
        out_shape=(
            jax.ShapeDtypeStruct((p_rows, LAT), jnp.bfloat16),
            jax.ShapeDtypeStruct((d_rows, LAT), jnp.bfloat16),
        ),
        in_specs=[smem, smem, anywhere, anywhere, anywhere, vmem],
        out_specs=(vmem, vmem),
        scratch_shapes=[
            pltpu.VMEM((ctx_count, 2, zs, rows, width), jnp.bfloat16),
            pltpu.VMEM((p_rows + d_rows, width), jnp.bfloat16),
            pltpu.VMEM((p_rows + d_rows, LAT), jnp.float32),
            pltpu.SemaphoreType.DMA((3,)),
            pltpu.SemaphoreType.DMA((copies,)),
            pltpu.SemaphoreType.DMA((ctx_count, 2, zs)),
        ],
        compiler_params=pltpu.CompilerParams(
            collective_id=0, has_side_effects=True, vmem_limit_bytes=48 * 1024 * 1024
        ),
        cost_estimate=pl.CostEstimate(
            flops=2 * pairs * (width + LAT), bytes_accessed=4 << 20, transcendentals=pairs
        ),
    )(
        lengths,
        group_of,
        latent,
        prefill_query.reshape(p_rows, width),
        decode_query.reshape(d_rows, width),
        own.reshape(steps * count, width),
    )
    return (
        prefill.reshape(q_count, heads, LAT),
        decode.reshape(1, steps, count, heads, LAT),
    )


def solution(mesh):
    in_specs = (
        P(("ctx", "ep"), None),
        P("ctx", "ep", None),
        P(),
        P(),
        P("ctx", None, None, None),
        P("ctx", None, None, "ep", None),
    )
    out_specs = (P("ctx", "ep", None), P("ctx", None, None, "ep", None))
    whole = functools.partial(body, mesh.shape["ctx"], mesh.shape["ep"])
    return jax.shard_map(whole, mesh=mesh, in_specs=in_specs, out_specs=out_specs, check_vma=False)
```

```python
import functools
import math

import jax
import jax.numpy as jnp
from jax import lax
from jax.experimental import pallas as pl
from jax.experimental.pallas import tpu as pltpu
from jax.sharding import PartitionSpec as P

LAT = 512
SCALE = 192 ** (-0.5)
RATE = SCALE * math.log2(math.e)
FLOOR = -1e30
MESH = pl.DeviceIdType.MESH


def layout(rows):
    halves = 2 if rows % 32 == 0 else 1
    return halves, 4 * rows + rows // halves


def kernel(
    sizes,
    lengths_ref,
    group_ref,
    latent_ref,
    pq_ref,
    dq_ref,
    own_ref,
    pout_ref,
    dout_ref,
    cache,
    pq_raw,
    dq_raw,
    queries,
    tails,
    acc,
    local_sem,
    send_sem,
    recv_sem,
):
    ctx_count, ep_count, heads, steps = sizes
    zs = ep_count // 2
    n2 = 2 if ctx_count % 2 == 0 else 1
    n1 = ctx_count // n2
    rows, width = latent_ref.shape
    halves, packed = layout(rows)
    half = rows // halves
    rope = width - LAT
    p_rows, d_rows = pout_ref.shape[0], dout_ref.shape[0]
    ctx = lax.axis_index("ctx")
    ep = lax.axis_index("ep")
    core = lax.rem(ep, 2)
    z = ep // 2
    i1, i2 = ctx // n2, lax.rem(ctx, n2)
    turn = core if n1 == n2 else 0
    na, nb = n2, n1
    line = zs == 4

    def column(a, b):
        o1 = b + turn * (a - b)
        o2 = a + turn * (b - a)
        return lax.rem(i1 + o1, n1) * n2 + lax.rem(i2 + o2, n2)

    flip = z // 2 if line else 0
    near = z + flip * (3 - 2 * z)

    def mirror(p):
        return p + flip * (3 - 2 * p)

    if line:
        planes = [z, mirror(1 - near), mirror(2), mirror(3)]
    else:
        planes = [lax.rem(z + dz, zs) for dz in range(zs)]

    def there(p):
        return (ctx, p * 2 + core)

    sibling = (ctx, ep + 1 - 2 * core)
    z_peers = [there(p) for p in planes[1:]]
    a_peers = [(column(a, 0), ep) for a in range(1, na)]
    b_peers = [(column(0, b), ep) for b in range(1, nb)]

    barrier = pltpu.get_barrier_semaphore()
    partners = [sibling] + z_peers + a_peers + b_peers
    for peer in partners:
        pl.semaphore_signal(barrier, inc=1, device_id=peer, device_id_type=MESH)

    p_copy = pltpu.make_async_copy(pq_ref, pq_raw, local_sem.at[0])
    p_copy.start()
    d_copy = pltpu.make_async_copy(dq_ref, dq_raw, local_sem.at[1])
    d_copy.start()
    for j in range(LAT // 128):
        cache[ctx, ep, pl.ds(j * rows, rows), :] = latent_ref[:, j * 128 : (j + 1) * 128]
    last = latent_ref[:, LAT:]
    if halves == 2:
        last = jnp.concatenate([last[:half], last[half:]], axis=1)
    else:
        last = jnp.concatenate([last, jnp.zeros_like(last)], axis=1)
    cache[ctx, ep, pl.ds(4 * rows, half), :] = last
    pl.semaphore_wait(barrier, len(partners))

    sent, sent_inner, used = [], [], [0]

    def link(col, index, peer):
        slot = cache.at[col, index]
        copy = pltpu.make_async_remote_copy(
            src_ref=slot,
            dst_ref=slot,
            send_sem=send_sem.at[used[0]],
            recv_sem=recv_sem.at[col, index],
            device_id=peer,
            device_id_type=MESH,
        )
        used[0] += 1
        return copy

    def landed(col, index):
        slot = cache.at[col, index]
        pltpu.make_async_remote_copy(
            src_ref=slot,
            dst_ref=slot,
            send_sem=send_sem.at[0],
            recv_sem=recv_sem.at[col, index],
            device_id=sibling,
            device_id_type=MESH,
        ).wait_recv()

    def forward(col, index, peers):
        for peer in peers:
            sent.append(link(col, index, peer))
            sent[-1].start()

    inner = near == 1
    if line:
        forward(ctx, ep, [there(mirror(near + 1))])
        sent_inner.append(link(ctx, ep, there(mirror(0))))
        pl.when(inner)(sent_inner[-1].start)
    else:
        forward(ctx, ep, z_peers)
    forward(ctx, ep, a_peers + b_peers + [sibling])

    def pass_on(col, i, peers):
        index = planes[i] * 2 + core
        landed(col, index)
        if line and col is ctx:
            goal = 2 if i == 1 else 0
            sent_inner.append(link(ctx, index, there(mirror(goal))))
            pl.when(inner)(sent_inner[-1].start)
        forward(col, index, peers)

    def await_sibling(col):
        for p in planes:
            landed(col, p * 2 + 1 - core)

    p_copy.wait()
    d_copy.wait()
    blank = jnp.zeros((p_rows, rope), jnp.bfloat16)
    block = p_rows
    blocks = (p_rows + d_rows) // block
    for i in range(blocks):
        if i == 0:
            raw = pq_raw[...]
        else:
            tokens = block // heads
            raw = dq_raw[pl.ds((i - 1) * tokens, tokens), :, :]
        raw = raw.reshape(block, width)
        at = pl.ds(i * block, block)
        queries[at, :] = raw[:, :LAT]
        tails[0, at, :] = jnp.concatenate([raw[:, LAT:], blank], axis=1)
        if halves == 2:
            tails[1, at, :] = jnp.concatenate([blank, raw[:, LAT:]], axis=1)

    request_count = lengths_ref.shape[0]
    q_count = p_rows // heads
    span = q_count * ctx_count // request_count
    chosen = group_ref[ctx]
    row = lax.broadcasted_iota(jnp.int32, (p_rows, 1), 0)
    query_id = ctx * q_count + row // heads
    low = jnp.zeros((p_rows, 1), jnp.int32)
    high = jnp.zeros((p_rows, 1), jnp.int32)
    d_low = jnp.int32(0)
    d_high = jnp.int32(0)
    end = jnp.int32(0)
    for r in range(request_count):
        start = end
        end = start + lengths_ref[r]
        mine = (query_id >= r * span) & (query_id < (r + 1) * span)
        low = jnp.where(mine, start, low)
        high = jnp.where(mine, end - span + (query_id - r * span), high)
        d_low = jnp.where(chosen == r, start, d_low)
        d_high = jnp.where(chosen == r, end, d_high)

    tops = [None] * blocks
    totals = [None] * blocks

    def lanes(x):
        out = x[:, :128]
        for i in range(1, x.shape[1] // 128):
            out = out + x[:, i * 128 : (i + 1) * 128]
        return out

    def attend(i, keys, values, allowed):
        at = pl.ds(i * block, block)
        scores = []
        for h, part in enumerate(keys):
            query = jnp.concatenate([queries[at, :], tails[h, at, :]], axis=1)
            scores.append(
                lax.dot_general(
                    query, part, (((1,), (1,)), ((), ())), preferred_element_type=jnp.float32
                )
            )
        scores = scores[0] if len(scores) == 1 else jnp.concatenate(scores, axis=1)
        scores = jnp.where(allowed, scores, FLOOR)
        top = jnp.max(scores, axis=1, keepdims=True)
        if tops[i] is not None:
            top = jnp.maximum(top, tops[i])
        weights = jnp.exp2((scores - top) * RATE)
        mixed = jnp.dot(
            weights.astype(jnp.bfloat16), values, preferred_element_type=jnp.float32
        )
        total = lanes(weights)
        if tops[i] is None:
            acc[at, :] = mixed
        else:
            keep = jnp.exp2((tops[i] - top) * RATE)
            acc[at, :] = acc[at, :] * keep + mixed
            total = total + totals[i] * keep
        tops[i], totals[i] = top, total

    def compute(col):
        keys, values = [], []
        count = ep_count * half
        for h in range(halves):
            tiles = [
                cache[col, :, pl.ds(j * rows + h * half, half), :].reshape(count, 128)
                for j in range(LAT // 128)
            ]
            tiles.append(cache[col, :, pl.ds(4 * rows, half), :].reshape(count, 128))
            keys.append(jnp.concatenate(tiles, axis=1))
            values.append(keys[-1][:, :LAT])
        values = values[0] if halves == 1 else jnp.concatenate(values, axis=0)
        lane = lax.broadcasted_iota(jnp.int32, (1, halves * count), 1)
        within = lane % count
        pos = (within // half) * rows + (lane // count) * half + within % half
        pos = pos + col * (rows * ep_count)
        attend(0, keys, values, (pos >= low) & (pos <= high))
        live = (pos >= d_low) & (pos < d_high)
        for i in range(1, blocks):
            attend(i, keys, values, live)

    def own_rows():
        count = own_ref.shape[0] // steps
        lane = lax.broadcasted_iota(jnp.int32, (1, own_ref.shape[0]), 1)
        own = own_ref[...]
        own_keys = jnp.concatenate([own, jnp.zeros((own.shape[0], rope), jnp.bfloat16)], axis=1)
        for i in range(1, blocks):
            at = lax.broadcasted_iota(jnp.int32, (block, 1), 0) + (i - 1) * block
            token = at // heads
            same = (lane % count == token % count) & (lane // count <= token // count)
            attend(i, [own_keys], own[:, :LAT], same)

    first = [(a, 0) for a in range(1, na)]
    second = [(0, b) for b in range(1, nb)]
    third = [(a, b) for b in range(1, nb) for a in range(1, na)]
    for i in range(zs + 1):
        if 1 <= i < zs:
            pass_on(ctx, i, a_peers + b_peers + [sibling])
        if i >= 1:
            for a, b in first:
                pass_on(column(a, b), i - 1, b_peers + [sibling])
        if i == 1:
            own_rows()
    await_sibling(ctx)
    compute(ctx)
    for a, b in second:
        for i in range(zs):
            pass_on(column(a, b), i, [sibling])
    for a, b in second + first:
        await_sibling(column(a, b))
        compute(column(a, b))
    for a, b in third:
        for i in range(zs):
            pass_on(column(a, b), i, [sibling])
        await_sibling(column(a, b))
        compute(column(a, b))

    for i in range(blocks):
        total = jnp.sum(totals[i], axis=1, keepdims=True)
        out = (acc[pl.ds(i * block, block), :] / total).astype(jnp.bfloat16)
        if i == 0:
            pout_ref[...] = out
        else:
            dout_ref[pl.ds((i - 1) * block, block), :] = out
    for copy in sent:
        copy.wait_send()
    for copy in sent_inner:
        pl.when(inner)(copy.wait_send)


def body(ctx_count, ep_count, latent, prefill_query, lengths, group_of, own, decode_query):
    rows, width = latent.shape
    q_count, heads, _ = prefill_query.shape
    _, steps, count, _, _ = decode_query.shape
    p_rows, d_rows = q_count * heads, steps * count * heads
    all_rows = p_rows + d_rows
    zs = ep_count // 2
    n2 = 2 if ctx_count % 2 == 0 else 1
    n1 = ctx_count // n2
    halves, packed = layout(rows)
    copies = 2 * zs + zs * ((n2 - 1) + n2 * (n1 - 1) + ctx_count)
    smem = pl.BlockSpec(memory_space=pltpu.SMEM)
    anywhere = pl.BlockSpec(memory_space=pl.ANY)
    vmem = pl.BlockSpec(memory_space=pltpu.VMEM)
    pairs = all_rows * (rows * ep_count * ctx_count + steps * count)
    prefill, decode = pl.pallas_call(
        functools.partial(kernel, (ctx_count, ep_count, heads, steps)),
        out_shape=(
            jax.ShapeDtypeStruct((p_rows, LAT), jnp.bfloat16),
            jax.ShapeDtypeStruct((d_rows, LAT), jnp.bfloat16),
        ),
        in_specs=[smem, smem, vmem, anywhere, anywhere, vmem],
        out_specs=(vmem, vmem),
        scratch_shapes=[
            pltpu.VMEM((ctx_count, ep_count, packed, 128), jnp.bfloat16),
            pltpu.VMEM((q_count, heads, width), jnp.bfloat16),
            pltpu.VMEM((steps * count, heads, width), jnp.bfloat16),
            pltpu.VMEM((all_rows, LAT), jnp.bfloat16),
            pltpu.VMEM((halves, all_rows, 128), jnp.bfloat16),
            pltpu.VMEM((all_rows, LAT), jnp.float32),
            pltpu.SemaphoreType.DMA((2,)),
            pltpu.SemaphoreType.DMA((copies,)),
            pltpu.SemaphoreType.DMA((ctx_count, ep_count)),
        ],
        compiler_params=pltpu.CompilerParams(
            collective_id=0, has_side_effects=True, vmem_limit_bytes=48 * 1024 * 1024
        ),
        cost_estimate=pl.CostEstimate(
            flops=2 * pairs * (width + LAT), bytes_accessed=4 << 20, transcendentals=pairs
        ),
    )(
        lengths,
        group_of,
        latent,
        prefill_query,
        decode_query.reshape(steps * count, heads, width),
        own.reshape(steps * count, width),
    )
    return (
        prefill.reshape(q_count, heads, LAT),
        decode.reshape(1, steps, count, heads, LAT),
    )


def solution(mesh):
    in_specs = (
        P(("ctx", "ep"), None),
        P("ctx", "ep", None),
        P(),
        P(),
        P("ctx", None, None, None),
        P("ctx", None, None, "ep", None),
    )
    out_specs = (P("ctx", "ep", None), P("ctx", None, None, "ep", None))
    whole = functools.partial(body, mesh.shape["ctx"], mesh.shape["ep"])
    return jax.shard_map(whole, mesh=mesh, in_specs=in_specs, out_specs=out_specs, check_vma=False)
```

```python
import functools
import math

import jax
import jax.numpy as jnp
from jax import lax
from jax.experimental import pallas as pl
from jax.experimental.pallas import tpu as pltpu
from jax.sharding import PartitionSpec as P

LAT = 512
SCALE = 192 ** (-0.5)
RATE = SCALE * math.log2(math.e)
FLOOR = -1e30
MESH = pl.DeviceIdType.MESH


def layout(rows):
    subs = 2 if rows % 64 == 0 else 1
    rows = rows // subs
    halves = 2 if rows % 32 == 0 else 1
    return subs, halves, 4 * rows + rows // halves


def kernel(
    sizes,
    lengths_ref,
    group_ref,
    latent_ref,
    pq_ref,
    dq_ref,
    own_ref,
    pout_ref,
    dout_ref,
    cache,
    latent_raw,
    own_raw,
    pq_raw,
    dq_raw,
    queries,
    tails,
    acc,
    local_sem,
    send_sem,
    recv_sem,
):
    ctx_count, ep_count, heads, steps = sizes
    zs = ep_count // 2
    n2 = 2 if ctx_count % 2 == 0 else 1
    n1 = ctx_count // n2
    shard, width = latent_ref.shape
    subs, halves, packed = layout(shard)
    rows = shard // subs
    half = rows // halves
    rope = width - LAT
    p_rows, d_rows = pout_ref.shape[0], dout_ref.shape[0]
    ctx = lax.axis_index("ctx")
    ep = lax.axis_index("ep")
    core = lax.rem(ep, 2)
    z = ep // 2
    i1, i2 = ctx // n2, lax.rem(ctx, n2)
    turn = core if n1 == n2 else 0
    na, nb = n2, n1
    line = zs == 4

    def column(a, b):
        o1 = b + turn * (a - b)
        o2 = a + turn * (b - a)
        return lax.rem(i1 + o1, n1) * n2 + lax.rem(i2 + o2, n2)

    flip = z // 2 if line else 0
    near = z + flip * (3 - 2 * z)

    def mirror(p):
        return p + flip * (3 - 2 * p)

    if line:
        planes = [z, mirror(1 - near), mirror(2), mirror(3)]
    else:
        planes = [lax.rem(z + dz, zs) for dz in range(zs)]

    def there(p):
        return (ctx, p * 2 + core)

    sibling = (ctx, ep + 1 - 2 * core)
    z_peers = [there(p) for p in planes[1:]]
    a_peers = [(column(a, 0), ep) for a in range(1, na)]
    b_peers = [(column(0, b), ep) for b in range(1, nb)]

    barrier = pltpu.get_barrier_semaphore()
    partners = [sibling] + z_peers + a_peers + b_peers
    for peer in partners:
        pl.semaphore_signal(barrier, inc=1, device_id=peer, device_id_type=MESH)

    copies = [
        pltpu.make_async_copy(source, target, local_sem.at[i])
        for i, (source, target) in enumerate(
            [(latent_ref, latent_raw), (pq_ref, pq_raw), (dq_ref, dq_raw), (own_ref, own_raw)]
        )
    ]
    for copy in copies:
        copy.start()
    copies[0].wait()
    for sub in range(subs):
        base = sub * rows
        for j in range(LAT // 128):
            tile = latent_raw[base : base + rows, j * 128 : (j + 1) * 128]
            cache[sub, ctx, ep, pl.ds(j * rows, rows), :] = tile
        last = latent_raw[base : base + rows, LAT:]
        if halves == 2:
            last = jnp.concatenate([last[:half], last[half:]], axis=1)
        else:
            last = jnp.concatenate([last, jnp.zeros_like(last)], axis=1)
        cache[sub, ctx, ep, pl.ds(4 * rows, half), :] = last
    pl.semaphore_wait(barrier, len(partners))

    sent = []

    def link(sub, col, index, peer):
        slot = cache.at[sub, col, index]
        return pltpu.make_async_remote_copy(
            src_ref=slot,
            dst_ref=slot,
            send_sem=send_sem.at[len(sent)],
            recv_sem=recv_sem.at[sub, col, index],
            device_id=peer,
            device_id_type=MESH,
        )

    def landed(sub, col, index):
        slot = cache.at[sub, col, index]
        pltpu.make_async_remote_copy(
            src_ref=slot,
            dst_ref=slot,
            send_sem=send_sem.at[0],
            recv_sem=recv_sem.at[sub, col, index],
            device_id=sibling,
            device_id_type=MESH,
        ).wait_recv()

    def forward(sub, col, index, peers):
        for peer in peers:
            sent.append(link(sub, col, index, peer))
            sent[-1].start()

    forward(0, ctx, ep, z_peers)
    early = list(sent)
    for sub in range(subs):
        forward(sub, ctx, ep, a_peers + b_peers + [sibling])

    def pass_on(sub, col, i, peers):
        index = planes[i] * 2 + core
        landed(sub, col, index)
        forward(sub, col, index, peers)

    def await_sibling(sub, col):
        for p in planes:
            landed(sub, col, p * 2 + 1 - core)

    for copy in copies[1:]:
        copy.wait()
    blank = jnp.zeros((p_rows, rope), jnp.bfloat16)
    block = p_rows
    blocks = (p_rows + d_rows) // block
    for i in range(blocks):
        if i == 0:
            raw = pq_raw[...]
        else:
            tokens = block // heads
            raw = dq_raw[pl.ds((i - 1) * tokens, tokens), :, :]
        raw = raw.reshape(block, width)
        at = pl.ds(i * block, block)
        queries[at, :] = raw[:, :LAT]
        tails[0, at, :] = jnp.concatenate([raw[:, LAT:], blank], axis=1)
        if halves == 2:
            tails[1, at, :] = jnp.concatenate([blank, raw[:, LAT:]], axis=1)

    request_count = lengths_ref.shape[0]
    q_count = p_rows // heads
    span = q_count * ctx_count // request_count
    chosen = group_ref[ctx]
    row = lax.broadcasted_iota(jnp.int32, (p_rows, 1), 0)
    query_id = ctx * q_count + row // heads
    low = jnp.zeros((p_rows, 1), jnp.int32)
    high = jnp.zeros((p_rows, 1), jnp.int32)
    d_low = jnp.int32(0)
    d_high = jnp.int32(0)
    end = jnp.int32(0)
    for r in range(request_count):
        start = end
        end = start + lengths_ref[r]
        mine = (query_id >= r * span) & (query_id < (r + 1) * span)
        low = jnp.where(mine, start, low)
        high = jnp.where(mine, end - span + (query_id - r * span), high)
        d_low = jnp.where(chosen == r, start, d_low)
        d_high = jnp.where(chosen == r, end, d_high)

    tops = [None] * blocks
    totals = [None] * blocks

    def lanes(x):
        out = x[:, :128]
        for i in range(1, x.shape[1] // 128):
            out = out + x[:, i * 128 : (i + 1) * 128]
        return out

    def attend(i, keys, values, allowed):
        at = pl.ds(i * block, block)
        scores = []
        for h, part in enumerate(keys):
            query = jnp.concatenate([queries[at, :], tails[h, at, :]], axis=1)
            scores.append(
                lax.dot_general(
                    query, part, (((1,), (1,)), ((), ())), preferred_element_type=jnp.float32
                )
            )
        scores = scores[0] if len(scores) == 1 else jnp.concatenate(scores, axis=1)
        scores = jnp.where(allowed, scores, FLOOR)
        top = jnp.max(scores, axis=1, keepdims=True)
        if tops[i] is not None:
            top = jnp.maximum(top, tops[i])
        weights = jnp.exp2((scores - top) * RATE)
        mixed = jnp.dot(
            weights.astype(jnp.bfloat16), values, preferred_element_type=jnp.float32
        )
        total = lanes(weights)
        if tops[i] is None:
            acc[at, :] = mixed
        else:
            keep = jnp.exp2((tops[i] - top) * RATE)
            acc[at, :] = acc[at, :] * keep + mixed
            total = total + totals[i] * keep
        tops[i], totals[i] = top, total

    def compute(items):
        keys, values, pos = [], [], []
        count = ep_count * half
        lane = lax.broadcasted_iota(jnp.int32, (1, count), 1)
        within = (lane // half) * shard + lane % half

        def tile(sub, col, first):
            return cache[sub, col, :, pl.ds(first, half), :].reshape(count, 128)

        for h in range(halves):
            blocks_of = []
            for sub, col in items:
                tiles = [tile(sub, col, j * rows + h * half) for j in range(LAT // 128)]
                tiles.append(tile(sub, col, 4 * rows))
                blocks_of.append(jnp.concatenate(tiles, axis=1))
                pos.append(within + (col * (shard * ep_count) + sub * rows + h * half))
            both = blocks_of[0] if len(blocks_of) == 1 else jnp.concatenate(blocks_of, axis=0)
            keys.append(both)
            values.append(both[:, :LAT])
        values = values[0] if halves == 1 else jnp.concatenate(values, axis=0)
        pos = pos[0] if len(pos) == 1 else jnp.concatenate(pos, axis=1)
        attend(0, keys, values, (pos >= low) & (pos <= high))
        live = (pos >= d_low) & (pos < d_high)
        for i in range(1, blocks):
            attend(i, keys, values, live)

    def own_rows():
        count = own_raw.shape[0] // steps
        lane = lax.broadcasted_iota(jnp.int32, (1, own_raw.shape[0]), 1)
        own = own_raw[...]
        own_keys = jnp.concatenate([own, jnp.zeros((own.shape[0], rope), jnp.bfloat16)], axis=1)
        for i in range(1, blocks):
            at = lax.broadcasted_iota(jnp.int32, (block, 1), 0) + (i - 1) * block
            token = at // heads
            same = (lane % count == token % count) & (lane // count <= token // count)
            attend(i, [own_keys], own[:, :LAT], same)

    first = [(a, 0) for a in range(1, na)]
    second = [(0, b) for b in range(1, nb)]
    third = [(a, b) for b in range(1, nb) for a in range(1, na)]
    def planes_in(sub):
        for i in range(1, zs):
            pass_on(sub, ctx, i, a_peers + b_peers + [sibling])

    def columns_in(sub, where, peers):
        for a, b in where:
            for i in range(zs):
                pass_on(sub, column(a, b), i, peers)

    def ready(items):
        for sub, col in items:
            await_sibling(sub, col)
        compute(items)

    own_rows()
    for copy in early:
        copy.wait_send()
    for sub in range(1, subs):
        forward(sub, ctx, ep, z_peers)
    planes_in(0)
    if subs == 2 and len(first) == len(second) == len(third) == 1:
        fa, fb, fc = column(*first[0]), column(*second[0]), column(*third[0])
        ready([(0, ctx)])
        planes_in(1)
        columns_in(0, first, b_peers + [sibling])
        ready([(1, ctx)])
        columns_in(0, second, [sibling])
        ready([(0, fa), (0, fb)])
        columns_in(1, first, b_peers + [sibling])
        columns_in(0, third, [sibling])
        columns_in(1, second, [sibling])
        ready([(0, fc), (1, fa), (1, fb)])
        columns_in(1, third, [sibling])
        ready([(1, fc)])
    else:
        for sub in range(1, subs):
            planes_in(sub)
        for sub in range(subs):
            columns_in(sub, first, b_peers + [sibling])
        for sub in range(subs):
            columns_in(sub, second + third, [sibling])
        ready([(sub, ctx) for sub in range(subs)])
        for a, b in first + second + third:
            ready([(sub, column(a, b)) for sub in range(subs)])

    for i in range(blocks):
        total = jnp.sum(totals[i], axis=1, keepdims=True)
        out = (acc[pl.ds(i * block, block), :] / total).astype(jnp.bfloat16)
        if i == 0:
            pout_ref[...] = out
        else:
            dout_ref[pl.ds((i - 1) * block, block), :] = out
    for copy in sent[len(early) :]:
        copy.wait_send()


def body(ctx_count, ep_count, latent, prefill_query, lengths, group_of, own, decode_query):
    rows, width = latent.shape
    q_count, heads, _ = prefill_query.shape
    _, steps, count, _, _ = decode_query.shape
    p_rows, d_rows = q_count * heads, steps * count * heads
    all_rows = p_rows + d_rows
    zs = ep_count // 2
    n2 = 2 if ctx_count % 2 == 0 else 1
    n1 = ctx_count // n2
    subs, halves, packed = layout(rows)
    copies = subs * zs * (n2 + n2 * (n1 - 1) + ctx_count)
    smem = pl.BlockSpec(memory_space=pltpu.SMEM)
    anywhere = pl.BlockSpec(memory_space=pl.ANY)
    vmem = pl.BlockSpec(memory_space=pltpu.VMEM)
    pairs = all_rows * (rows * ep_count * ctx_count + steps * count)
    prefill, decode = pl.pallas_call(
        functools.partial(kernel, (ctx_count, ep_count, heads, steps)),
        out_shape=(
            jax.ShapeDtypeStruct((p_rows, LAT), jnp.bfloat16),
            jax.ShapeDtypeStruct((d_rows, LAT), jnp.bfloat16),
        ),
        in_specs=[smem, smem] + [anywhere] * 4,
        out_specs=(vmem, vmem),
        scratch_shapes=[
            pltpu.VMEM((subs, ctx_count, ep_count, packed, 128), jnp.bfloat16),
            pltpu.VMEM((rows, width), jnp.bfloat16),
            pltpu.VMEM((steps * count, width), jnp.bfloat16),
            pltpu.VMEM((q_count, heads, width), jnp.bfloat16),
            pltpu.VMEM((steps * count, heads, width), jnp.bfloat16),
            pltpu.VMEM((all_rows, LAT), jnp.bfloat16),
            pltpu.VMEM((halves, all_rows, 128), jnp.bfloat16),
            pltpu.VMEM((all_rows, LAT), jnp.float32),
            pltpu.SemaphoreType.DMA((4,)),
            pltpu.SemaphoreType.DMA((copies,)),
            pltpu.SemaphoreType.DMA((subs, ctx_count, ep_count)),
        ],
        compiler_params=pltpu.CompilerParams(
            collective_id=0, has_side_effects=True, vmem_limit_bytes=60 * 1024 * 1024
        ),
        cost_estimate=pl.CostEstimate(
            flops=2 * pairs * (width + LAT), bytes_accessed=4 << 20, transcendentals=pairs
        ),
    )(
        lengths,
        group_of,
        latent,
        prefill_query,
        decode_query.reshape(steps * count, heads, width),
        own.reshape(steps * count, width),
    )
    return (
        prefill.reshape(q_count, heads, LAT),
        decode.reshape(1, steps, count, heads, LAT),
    )


def solution(mesh):
    in_specs = (
        P(("ctx", "ep"), None),
        P("ctx", "ep", None),
        P(),
        P(),
        P("ctx", None, None, None),
        P("ctx", None, None, "ep", None),
    )
    out_specs = (P("ctx", "ep", None), P("ctx", None, None, "ep", None))
    whole = functools.partial(body, mesh.shape["ctx"], mesh.shape["ep"])
    return jax.shard_map(whole, mesh=mesh, in_specs=in_specs, out_specs=out_specs, check_vma=False)
```

```python
import functools
import math

import jax
import jax.numpy as jnp
from jax import lax
from jax.experimental import pallas as pl
from jax.experimental.pallas import tpu as pltpu
from jax.sharding import PartitionSpec as P

LAT = 512
SCALE = 192 ** (-0.5)
RATE = SCALE * math.log2(math.e)
FLOOR = -1e30
MESH = pl.DeviceIdType.MESH


def layout(rows):
    subs = 2 if rows % 64 == 0 else 1
    rows = rows // subs
    halves = 2 if rows % 32 == 0 else 1
    return subs, halves, 4 * rows + rows // halves


def kernel(
    sizes,
    lengths_ref,
    group_ref,
    latent_ref,
    pq_ref,
    dq_ref,
    own_ref,
    pout_ref,
    dout_ref,
    cache,
    latent_raw,
    own_raw,
    pq_raw,
    dq_raw,
    queries,
    tails,
    acc,
    local_sem,
    send_sem,
    recv_sem,
):
    ctx_count, ep_count, heads, steps = sizes
    zs = ep_count // 2
    n2 = 2 if ctx_count % 2 == 0 else 1
    n1 = ctx_count // n2
    shard, width = latent_ref.shape
    subs, halves, packed = layout(shard)
    rows = shard // subs
    half = rows // halves
    rope = width - LAT
    p_rows, d_rows = pout_ref.shape[0], dout_ref.shape[0]
    ctx = lax.axis_index("ctx")
    ep = lax.axis_index("ep")
    core = lax.rem(ep, 2)
    z = ep // 2
    i1, i2 = ctx // n2, lax.rem(ctx, n2)
    turn = core if n1 == n2 else 0
    na, nb = n2, n1
    line = zs == 4

    def column(a, b):
        o1 = b + turn * (a - b)
        o2 = a + turn * (b - a)
        return lax.rem(i1 + o1, n1) * n2 + lax.rem(i2 + o2, n2)

    flip = z // 2 if line else 0
    near = z + flip * (3 - 2 * z)

    def mirror(p):
        return p + flip * (3 - 2 * p)

    if line:
        planes = [z, mirror(1 - near), mirror(2), mirror(3)]
    else:
        planes = [lax.rem(z + dz, zs) for dz in range(zs)]

    def there(p):
        return (ctx, p * 2 + core)

    sibling = (ctx, ep + 1 - 2 * core)
    z_peers = [there(p) for p in planes[1:]]
    a_peers = [(column(a, 0), ep) for a in range(1, na)]
    b_peers = [(column(0, b), ep) for b in range(1, nb)]

    barrier = pltpu.get_barrier_semaphore()
    partners = [sibling] + z_peers + a_peers + b_peers
    for peer in partners:
        pl.semaphore_signal(barrier, inc=1, device_id=peer, device_id_type=MESH)

    copies = [
        pltpu.make_async_copy(source, target, local_sem.at[i])
        for i, (source, target) in enumerate(
            [(latent_ref, latent_raw), (pq_ref, pq_raw), (dq_ref, dq_raw), (own_ref, own_raw)]
        )
    ]
    for copy in copies:
        copy.start()
    copies[0].wait()
    for sub in range(subs):
        base = sub * rows
        for j in range(LAT // 128):
            tile = latent_raw[base : base + rows, j * 128 : (j + 1) * 128]
            cache[sub, ctx, ep, pl.ds(j * rows, rows), :] = tile
        last = latent_raw[base : base + rows, LAT:]
        if halves == 2:
            last = jnp.concatenate([last[:half], last[half:]], axis=1)
        else:
            last = jnp.concatenate([last, jnp.zeros_like(last)], axis=1)
        cache[sub, ctx, ep, pl.ds(4 * rows, half), :] = last
    pl.semaphore_wait(barrier, len(partners))

    sent = []

    def link(sub, col, index, peer):
        slot = cache.at[sub, col, index]
        return pltpu.make_async_remote_copy(
            src_ref=slot,
            dst_ref=slot,
            send_sem=send_sem.at[len(sent)],
            recv_sem=recv_sem.at[sub, col, index],
            device_id=peer,
            device_id_type=MESH,
        )

    def landed(sub, col, index):
        slot = cache.at[sub, col, index]
        pltpu.make_async_remote_copy(
            src_ref=slot,
            dst_ref=slot,
            send_sem=send_sem.at[0],
            recv_sem=recv_sem.at[sub, col, index],
            device_id=sibling,
            device_id_type=MESH,
        ).wait_recv()

    def forward(sub, col, index, peers):
        for peer in peers:
            sent.append(link(sub, col, index, peer))
            sent[-1].start()

    forward(0, ctx, ep, z_peers)
    early = list(sent)
    for sub in range(subs):
        forward(sub, ctx, ep, a_peers + b_peers + [sibling])

    def pass_on(sub, col, i, peers):
        index = planes[i] * 2 + core
        landed(sub, col, index)
        forward(sub, col, index, peers)

    def await_sibling(sub, col):
        for p in planes:
            landed(sub, col, p * 2 + 1 - core)

    for copy in copies[1:]:
        copy.wait()
    blank = jnp.zeros((p_rows, rope), jnp.bfloat16)
    block = p_rows
    blocks = (p_rows + d_rows) // block
    for i in range(blocks):
        if i == 0:
            raw = pq_raw[...]
        else:
            tokens = block // heads
            raw = dq_raw[pl.ds((i - 1) * tokens, tokens), :, :]
        raw = raw.reshape(block, width)
        at = pl.ds(i * block, block)
        queries[at, :] = raw[:, :LAT]
        tails[0, at, :] = jnp.concatenate([raw[:, LAT:], blank], axis=1)
        if halves == 2:
            tails[1, at, :] = jnp.concatenate([blank, raw[:, LAT:]], axis=1)

    request_count = lengths_ref.shape[0]
    q_count = p_rows // heads
    span = q_count * ctx_count // request_count
    chosen = group_ref[ctx]
    row = lax.broadcasted_iota(jnp.int32, (p_rows, 1), 0)
    query_id = ctx * q_count + row // heads
    low = jnp.zeros((p_rows, 1), jnp.int32)
    high = jnp.zeros((p_rows, 1), jnp.int32)
    d_low = jnp.int32(0)
    d_high = jnp.int32(0)
    end = jnp.int32(0)
    for r in range(request_count):
        start = end
        end = start + lengths_ref[r]
        mine = (query_id >= r * span) & (query_id < (r + 1) * span)
        low = jnp.where(mine, start, low)
        high = jnp.where(mine, end - span + (query_id - r * span), high)
        d_low = jnp.where(chosen == r, start, d_low)
        d_high = jnp.where(chosen == r, end, d_high)

    tops = [None] * blocks
    totals = [None] * blocks

    def lanes(x):
        out = x[:, :128]
        for i in range(1, x.shape[1] // 128):
            out = out + x[:, i * 128 : (i + 1) * 128]
        return out

    def attend(i, keys, values, allowed):
        at = pl.ds(i * block, block)
        scores = []
        for h, part in enumerate(keys):
            query = jnp.concatenate([queries[at, :], tails[h, at, :]], axis=1)
            scores.append(
                lax.dot_general(
                    query, part, (((1,), (1,)), ((), ())), preferred_element_type=jnp.float32
                )
            )
        scores = scores[0] if len(scores) == 1 else jnp.concatenate(scores, axis=1)
        scores = jnp.where(allowed, scores, FLOOR)
        top = jnp.max(scores, axis=1, keepdims=True)
        if tops[i] is not None:
            top = jnp.maximum(top, tops[i])
        weights = jnp.exp2((scores - top) * RATE)
        mixed = jnp.dot(
            weights.astype(jnp.bfloat16), values, preferred_element_type=jnp.float32
        )
        total = lanes(weights)
        if tops[i] is None:
            acc[at, :] = mixed
        else:
            keep = jnp.exp2((tops[i] - top) * RATE)
            acc[at, :] = acc[at, :] * keep + mixed
            total = total + totals[i] * keep
        tops[i], totals[i] = top, total

    def compute(items):
        keys, values, pos = [], [], []
        count = ep_count * half
        lane = lax.broadcasted_iota(jnp.int32, (1, count), 1)
        within = (lane // half) * shard + lane % half

        def tile(sub, col, first):
            return cache[sub, col, :, pl.ds(first, half), :].reshape(count, 128)

        for h in range(halves):
            blocks_of = []
            for sub, col in items:
                tiles = [tile(sub, col, j * rows + h * half) for j in range(LAT // 128)]
                tiles.append(tile(sub, col, 4 * rows))
                blocks_of.append(jnp.concatenate(tiles, axis=1))
                pos.append(within + (col * (shard * ep_count) + sub * rows + h * half))
            both = blocks_of[0] if len(blocks_of) == 1 else jnp.concatenate(blocks_of, axis=0)
            keys.append(both)
            values.append(both[:, :LAT])
        values = values[0] if halves == 1 else jnp.concatenate(values, axis=0)
        pos = pos[0] if len(pos) == 1 else jnp.concatenate(pos, axis=1)
        attend(0, keys, values, (pos >= low) & (pos <= high))
        live = (pos >= d_low) & (pos < d_high)
        for i in range(1, blocks):
            attend(i, keys, values, live)

    def own_rows():
        count = own_raw.shape[0] // steps
        lane = lax.broadcasted_iota(jnp.int32, (1, own_raw.shape[0]), 1)
        own = own_raw[...]
        own_keys = jnp.concatenate([own, jnp.zeros((own.shape[0], rope), jnp.bfloat16)], axis=1)
        for i in range(1, blocks):
            at = lax.broadcasted_iota(jnp.int32, (block, 1), 0) + (i - 1) * block
            token = at // heads
            same = (lane % count == token % count) & (lane // count <= token // count)
            attend(i, [own_keys], own[:, :LAT], same)

    first = [(a, 0) for a in range(1, na)]
    second = [(0, b) for b in range(1, nb)]
    third = [(a, b) for b in range(1, nb) for a in range(1, na)]
    def planes_in(sub):
        for i in range(1, zs):
            pass_on(sub, ctx, i, a_peers + b_peers + [sibling])

    def columns_in(sub, where, peers):
        for a, b in where:
            for i in range(zs):
                pass_on(sub, column(a, b), i, peers)

    def ready(items):
        for sub, col in items:
            await_sibling(sub, col)
        compute(items)

    own_rows()
    for copy in early:
        copy.wait_send()
    for sub in range(1, subs):
        forward(sub, ctx, ep, z_peers)
    planes_in(0)
    if subs == 2 and len(first) == len(second) == len(third) == 1:
        fa, fb, fc = column(*first[0]), column(*second[0]), column(*third[0])
        ready([(0, ctx)])
        planes_in(1)
        columns_in(0, first, b_peers + [sibling])
        ready([(1, ctx)])
        columns_in(0, second, [sibling])
        ready([(0, fa), (0, fb)])
        columns_in(1, first, b_peers + [sibling])
        columns_in(0, third, [sibling])
        columns_in(1, second, [sibling])
        ready([(0, fc), (1, fa), (1, fb)])
        columns_in(1, third, [sibling])
        ready([(1, fc)])
    else:
        for sub in range(1, subs):
            planes_in(sub)
        for sub in range(subs):
            columns_in(sub, first, b_peers + [sibling])
        for sub in range(subs):
            columns_in(sub, second + third, [sibling])
        ready([(sub, ctx) for sub in range(subs)])
        for a, b in first + second + third:
            ready([(sub, column(a, b)) for sub in range(subs)])

    for i in range(blocks):
        share = 1.0 / jnp.sum(totals[i], axis=1, keepdims=True)
        out = (acc[pl.ds(i * block, block), :] * share).astype(jnp.bfloat16)
        if i == 0:
            pout_ref[...] = out
        else:
            dout_ref[pl.ds((i - 1) * block, block), :] = out
    for copy in sent[len(early) :]:
        copy.wait_send()


def body(ctx_count, ep_count, latent, prefill_query, lengths, group_of, own, decode_query):
    rows, width = latent.shape
    q_count, heads, _ = prefill_query.shape
    _, steps, count, _, _ = decode_query.shape
    p_rows, d_rows = q_count * heads, steps * count * heads
    all_rows = p_rows + d_rows
    zs = ep_count // 2
    n2 = 2 if ctx_count % 2 == 0 else 1
    n1 = ctx_count // n2
    subs, halves, packed = layout(rows)
    copies = subs * zs * (n2 + n2 * (n1 - 1) + ctx_count)
    smem = pl.BlockSpec(memory_space=pltpu.SMEM)
    anywhere = pl.BlockSpec(memory_space=pl.ANY)
    vmem = pl.BlockSpec(memory_space=pltpu.VMEM)
    pairs = all_rows * (rows * ep_count * ctx_count + steps * count)
    prefill, decode = pl.pallas_call(
        functools.partial(kernel, (ctx_count, ep_count, heads, steps)),
        out_shape=(
            jax.ShapeDtypeStruct((p_rows, LAT), jnp.bfloat16),
            jax.ShapeDtypeStruct((d_rows, LAT), jnp.bfloat16),
        ),
        in_specs=[smem, smem] + [anywhere] * 4,
        out_specs=(vmem, vmem),
        scratch_shapes=[
            pltpu.VMEM((subs, ctx_count, ep_count, packed, 128), jnp.bfloat16),
            pltpu.VMEM((rows, width), jnp.bfloat16),
            pltpu.VMEM((steps * count, width), jnp.bfloat16),
            pltpu.VMEM((q_count, heads, width), jnp.bfloat16),
            pltpu.VMEM((steps * count, heads, width), jnp.bfloat16),
            pltpu.VMEM((all_rows, LAT), jnp.bfloat16),
            pltpu.VMEM((halves, all_rows, 128), jnp.bfloat16),
            pltpu.VMEM((all_rows, LAT), jnp.float32),
            pltpu.SemaphoreType.DMA((4,)),
            pltpu.SemaphoreType.DMA((copies,)),
            pltpu.SemaphoreType.DMA((subs, ctx_count, ep_count)),
        ],
        compiler_params=pltpu.CompilerParams(
            collective_id=0, has_side_effects=True, vmem_limit_bytes=60 * 1024 * 1024
        ),
        cost_estimate=pl.CostEstimate(
            flops=2 * pairs * (width + LAT), bytes_accessed=4 << 20, transcendentals=pairs
        ),
    )(
        lengths,
        group_of,
        latent,
        prefill_query,
        decode_query.reshape(steps * count, heads, width),
        own.reshape(steps * count, width),
    )
    return (
        prefill.reshape(q_count, heads, LAT),
        decode.reshape(1, steps, count, heads, LAT),
    )


def solution(mesh):
    in_specs = (
        P(("ctx", "ep"), None),
        P("ctx", "ep", None),
        P(),
        P(),
        P("ctx", None, None, None),
        P("ctx", None, None, "ep", None),
    )
    out_specs = (P("ctx", "ep", None), P("ctx", None, None, "ep", None))
    whole = functools.partial(body, mesh.shape["ctx"], mesh.shape["ep"])
    return jax.shard_map(whole, mesh=mesh, in_specs=in_specs, out_specs=out_specs, check_vma=False)
```
